32 devices in a mesh: subj: 8 (over z, core), vox: 4 (over y, x).
Axes of the slice: x: 2, y: 2, z: 4, core: 2. Of those that a mesh axis runs over, the one named last changes fastest.
Arguments:
- data: bfloat16 [16, 240, 16384], P('subj', None, 'vox'), may hold values from -40 to 40, as said below
- shared_start: bfloat16 [128, 240], replicated, may hold values from -6 to 6
Outputs:
- projections: float32 [16, 128, 240], P('subj')
- response: float32 [128, 240], replicated
The draws below stay inside these ranges and needn't reach their ends.
Inputs may be any that keep to these rules, and one draw needn't show every extreme that they name: `data`: real-valued recordings.
All inputs are finite; a program needn't handle non-finite values.
Results may differ from the reference program's by a relative error of at most 0.00035.
The reference program's roundings to bfloat16 on the way (of `shared`) count: a program that leaves them out, or rounds other values in their place, can miss the bound.
Values may be sent and summed in bfloat16 or wider, within the bound.
A program may use at most 64 MiB of HBM per device.

```python
import jax
import jax.numpy as jnp
from jax import lax

FEATURES = 128
FRAMES = 240
ITERS = 3
OUTER = 2
SUBJECTS = 16
VOXELS = 16384


def draw_data(key, part):
    first, second, third = jax.random.split(jax.random.fold_in(key, 11), 3)
    voxel_scale = 10.0 ** (jax.random.uniform(second, (SUBJECTS, 1, VOXELS), jnp.float32) - 0.5)
    frame_scale = 10.0 ** (jax.random.uniform(third, (SUBJECTS, FRAMES, 1), jnp.float32) - 0.5)
    base = jnp.clip(jax.random.normal(first, (SUBJECTS, FRAMES, VOXELS), jnp.float32), -4.0, 4.0)
    return (base * voxel_scale * frame_scale).astype(jnp.bfloat16)


def noise(own_key, dims, spread, bound, dtype=jnp.bfloat16):
    drawn = jax.random.normal(own_key, dims, jnp.float32) * spread
    return jnp.minimum(jnp.maximum(drawn, -bound), bound).astype(dtype)


def setup_inputs(seed: int = 0) -> dict:
    streams_of = jax.random.split(jax.random.key(seed), 3)
    return {
        "data": draw_data(jax.random.fold_in(streams_of[2], 71), 0),
        "shared_start": noise(streams_of[1], (FEATURES, FRAMES), 1.0, 6.0),
    }


def refit(record, shared):
    cross = jnp.dot(record.T, shared.T, preferred_element_type=jnp.float32)
    scale = jnp.sqrt(jnp.sum(cross * cross) + 1e-06)
    iterate = cross / scale
    for count in range(ITERS):
        gram = jnp.dot(iterate.T, iterate, precision=lax.Precision.HIGHEST)
        iterate = 1.5 * iterate - 0.5 * jnp.dot(iterate, gram, precision=lax.Precision.HIGHEST)
    return jnp.dot(iterate.T, record.T.astype(jnp.float32), precision=lax.Precision.HIGHEST)

def reference(data, shared_start):
    shared = shared_start
    projections = None
    response = None
    for outer in range(OUTER):
        projections = lax.map(lambda record: refit(record, shared), data)
        response = lax.optimization_barrier(jnp.sum(projections, axis=0)) / jnp.float32(SUBJECTS)
        shared = response.astype(jnp.bfloat16)
    return (projections, response)
```

```python
import functools

import jax
import jax.numpy as jnp
from jax import lax
from jax.experimental import pallas as pl
from jax.experimental.pallas import tpu as pltpu
from jax.sharding import PartitionSpec as P

OUTER = 2
LANES = 128
ROWS = 16
PIECES = 4
MESH = pl.DeviceIdType.MESH


def each(start, stop, body):
    if stop - start <= 16:
        for step in range(start, stop):
            body(step)
    else:

        def looped(step, carry):
            body(step)
            return carry

        lax.fori_loop(start, stop, looped, 0)


def halves(x):
    high = x.astype(jnp.bfloat16)
    low = (x - high.astype(jnp.float32)).astype(jnp.bfloat16)
    return high, low


def dot(x, y):
    return jnp.dot(x, y, preferred_element_type=jnp.float32)


def dot_t(x, y):
    return lax.dot_general(x, y, (((1,), (1,)), ((), ())), preferred_element_type=jnp.float32)


def product(x, y):
    x_high, x_low = x
    y_high, y_low = y
    wide = jnp.concatenate([x_high, x_low], axis=1)
    tall = jnp.concatenate([y_high, y_high], axis=0)
    return dot(wide, tall) + dot(x_high, y_low)


def chain(shared, grams):
    features = shared.shape[0]
    row = lax.broadcasted_iota(jnp.int32, (features, features), 0)
    col = lax.broadcasted_iota(jnp.int32, (features, features), 1)
    left = [dot(shared, high) + dot(shared, low) for high, low in grams]
    left2 = [halves(x) for x in left]
    first = [dot_t(high, shared) + dot_t(low, shared) for high, low in left2]
    squares = [jnp.sum(jnp.where(row == col, x, 0.0), keepdims=True) + 1e-06 for x in first]
    gram = [x * (1.0 / s) for x, s in zip(first, squares)]
    gram2 = [halves(x) for x in gram]
    for last in (False, False, True):
        if not last:
            square = [product(x, x) for x in gram2]
        left = [1.5 * x - 0.5 * product(g, y) for x, g, y in zip(left, gram2, left2)]
        if not last:
            square2 = [halves(x) for x in square]
            gram = [
                2.25 * g - 1.5 * q + 0.25 * product(g2, q2)
                for g, q, g2, q2 in zip(gram, square, gram2, square2)
            ]
            gram2 = [halves(x) for x in gram]
            left2 = [halves(x) for x in left]
    return [x * lax.rsqrt(s) for x, s in zip(left, squares)]


def pack(gram, frames, total_rows):
    rest = frames - LANES
    row = lax.broadcasted_iota(jnp.int32, (LANES, LANES), 0)
    col = lax.broadcasted_iota(jnp.int32, (LANES, LANES), 1)
    corner = gram[LANES:, LANES:]
    corner = jnp.concatenate([corner, jnp.zeros((rest, LANES - rest), jnp.float32)], axis=1)
    corner = jnp.concatenate([corner, jnp.zeros((LANES - rest, LANES), jnp.float32)], axis=0)
    corner = pltpu.roll(corner, 1, 1)
    parts = [jnp.where(row >= col, gram[:LANES, :LANES], corner), gram[LANES:, :LANES]]
    if total_rows > frames:
        parts.append(jnp.zeros((total_rows - frames, LANES), jnp.float32))
    return jnp.concatenate(parts, axis=0)


def unpack(packed, frames):
    rest = frames - LANES
    row = lax.broadcasted_iota(jnp.int32, (LANES, LANES), 0)
    col = lax.broadcasted_iota(jnp.int32, (LANES, LANES), 1)
    both = packed[:LANES]
    cross = packed[LANES:frames]
    cross = jnp.concatenate([cross, jnp.zeros((LANES - rest, LANES), jnp.float32)], axis=0)
    top = jnp.where(row >= col, both, both.T)
    rolled = pltpu.roll(both, LANES - 1, 1)
    corner = jnp.where(col >= row, rolled, rolled.T)
    corner = jnp.where((row < rest) & (col < rest), corner, 0.0)
    return jnp.concatenate(
        [jnp.concatenate([top, cross.T], axis=1), jnp.concatenate([cross, corner], axis=1)], axis=0
    )


def kernel(
    cores, subj_n, vox_n, chunk, subjects,
    data_ref, shared_ref, proj_ref, resp_ref,
    held, acc, packed, parts, gathered, tiles, sums, shares, pieces, proj_buf,
    load_sem, out_sem, rs_send, rs_recv, ag_send, ag_recv, sum_send, sum_recv, share_send, share_recv,
    piece_send, piece_recv,
):
    own, frames, voxels = data_ref.shape
    features = shared_ref.shape[0]
    s = lax.axis_index("subj")
    v = lax.axis_index("vox")
    z = s // cores
    core = s % cores
    planes = subj_n // cores
    chips = planes * vox_n
    chip = z * vox_n + v
    tile_n = (features // ROWS) * 2
    mine = chip

    def subj_device(step):
        return (lax.rem(s + step, subj_n), v)

    def chip_device(step):
        other = lax.rem(chip + step, chips)
        return (other // vox_n * cores + core, lax.rem(other, vox_n))

    def vox_device(step):
        return (s, lax.rem(v + step, vox_n))

    width = voxels // PIECES
    loads = []
    for i in range(own):
        for p in range(PIECES):
            cut = pl.ds(p * width, width)
            load = pltpu.make_async_copy(
                data_ref.at[i, :, cut], held.at[i, :, cut], load_sem.at[i, p]
            )
            load.start()
            loads.append(load)

    barrier = pltpu.get_barrier_semaphore()

    def greet_subj(step):
        pl.semaphore_signal(barrier, inc=1, device_id=subj_device(step), device_id_type=MESH)

    def greet_chip(step):
        pl.semaphore_signal(barrier, inc=1, device_id=chip_device(step), device_id_type=MESH)

    each(1, subj_n, greet_subj)
    each(1, chips, greet_chip)

    def scatter(i, step):
        other = lax.rem(v + step, vox_n)
        return pltpu.make_async_remote_copy(
            src_ref=packed.at[i, pl.ds(pl.multiple_of(other * chunk, 8), chunk)],
            dst_ref=parts.at[i, step - 1],
            send_sem=rs_send.at[i, step - 1],
            recv_sem=rs_recv.at[i, step - 1],
            device_id=vox_device(step),
            device_id_type=MESH,
        )

    def gather(i, step):
        cut = pl.ds(pl.multiple_of(v * chunk, 8), chunk)
        return pltpu.make_async_remote_copy(
            src_ref=gathered.at[i, cut],
            dst_ref=gathered.at[i, cut],
            send_sem=ag_send.at[i, step - 1],
            recv_sem=ag_recv.at[i, step - 1],
            device_id=vox_device(step),
            device_id_type=MESH,
        )

    def sum_copy(o, step):
        other = lax.rem(s + step, subj_n)
        tile = jnp.minimum(other // cores * vox_n + v, tile_n - 1)
        return pltpu.make_async_remote_copy(
            src_ref=tiles.at[o, tile],
            dst_ref=sums.at[o, s],
            send_sem=sum_send.at[o, step - 1],
            recv_sem=sum_recv.at[o, step - 1],
            device_id=subj_device(step),
            device_id_type=MESH,
        )

    def share_copy(o, step):
        ref = pieces if o else shares
        tile = jnp.minimum(mine, tile_n - 1)
        return pltpu.make_async_remote_copy(
            src_ref=ref.at[tile],
            dst_ref=ref.at[tile],
            send_sem=(piece_send if o else share_send).at[step - 1],
            recv_sem=(piece_recv if o else share_recv).at[step - 1],
            device_id=chip_device(step),
            device_id_type=MESH,
        )

    def when(condition, body):
        if chips <= tile_n:
            body()
        else:
            pl.when(condition)(body)

    for i in range(own):
        for p in range(PIECES):
            loads[i * PIECES + p].wait()
            piece = held[i, :, p * width : (p + 1) * width]
            if p == 0:
                acc[...] = dot_t(piece, piece)
            else:
                acc[...] += dot_t(piece, piece)
        packed[i] = pack(acc[...], frames, vox_n * chunk)
        if i == 0:
            pl.semaphore_wait(barrier, subj_n - 1 + chips - 1)
        each(1, vox_n, lambda step: scatter(i, step).start())

    for i in range(own):
        each(1, vox_n, lambda step: scatter(i, step).wait_recv())
        total = packed[i, pl.ds(pl.multiple_of(v * chunk, 8), chunk)]
        for step in range(1, vox_n):
            total = total + parts[i, step - 1]
        gathered[i, pl.ds(pl.multiple_of(v * chunk, 8), chunk)] = total
        each(1, vox_n, lambda step: gather(i, step).start())

    grams = []
    for i in range(own):
        each(1, vox_n, lambda step: gather(i, step).wait_recv())
        grams.append(halves(unpack(gathered[i], frames)))

    shared = shared_ref[...]
    pad = jnp.zeros((features, 2 * LANES - frames), jnp.bfloat16)
    shared = jnp.concatenate([shared, pad], axis=1)

    for o in range(OUTER):
        projections = chain(shared, grams)
        total = projections[0]
        for other in projections[1:]:
            total = total + other
        for j in range(tile_n):
            tiles[o, j] = total[
                j // 2 * ROWS : (j // 2 + 1) * ROWS, j % 2 * LANES : (j % 2 + 1) * LANES
            ]

        def send_sum(step):
            other = lax.rem(s + step, subj_n)
            when(
                other // cores * vox_n + v < tile_n,
                lambda: sum_copy(o, step).start(),
            )

        each(1, subj_n, send_sum)
        if o == OUTER - 1:
            for i in range(own):
                proj_buf[i] = projections[i][:, :frames]
            writing = pltpu.make_async_copy(proj_buf, proj_ref, out_sem)
            writing.start()

        def reduce():
            sums[o, s] = tiles[o, mine]
            each(1, subj_n, lambda step: sum_copy(o, step).wait_recv())
            summed = sums[o, 0]
            for q in range(1, subj_n):
                summed = summed + sums[o, q]
            mean = summed / jnp.float32(subjects)
            if o == OUTER - 1:
                pieces[mine] = mean
            else:
                shares[mine] = mean.astype(jnp.bfloat16)
            each(1, chips, lambda step: share_copy(o, step).start())

        when(mine < tile_n, reduce)

        def wait_share(step):
            other = lax.rem(chip + chips - step, chips)
            when(other < tile_n, lambda: share_copy(o, step).wait_recv())

        each(1, chips, wait_share)
        ref = pieces if o == OUTER - 1 else shares
        shared = jnp.concatenate(
            [
                jnp.concatenate([ref[2 * a], ref[2 * a + 1]], axis=1)
                for a in range(tile_n // 2)
            ],
            axis=0,
        )
    resp_ref[...] = shared[:, :frames]

    for i in range(own):
        each(1, vox_n, lambda step: scatter(i, step).wait_send())
        each(1, vox_n, lambda step: gather(i, step).wait_send())
    for o in range(OUTER):

        def sent_sum(step):
            other = lax.rem(s + step, subj_n)
            when(
                other // cores * vox_n + v < tile_n,
                lambda: sum_copy(o, step).wait_send(),
            )

        each(1, subj_n, sent_sum)
        when(
            mine < tile_n,
            lambda: each(1, chips, lambda step: share_copy(o, step).wait_send()),
        )
    writing.wait()


def local(subj_n, vox_n, data, shared_start):
    own, frames, voxels = data.shape
    features = shared_start.shape[0]
    cores = 2
    chips = subj_n // cores * vox_n
    tile_n = features // ROWS * 2
    assert chips >= tile_n and tile_n % vox_n == 0
    chunk = -(-frames // (8 * vox_n)) * 8
    hbm = pl.BlockSpec(memory_space=pltpu.HBM)
    vmem = pl.BlockSpec(memory_space=pltpu.VMEM)
    f32, bf16 = jnp.float32, jnp.bfloat16
    dma = pltpu.SemaphoreType.DMA
    flops = 2 * own * frames * frames * voxels
    return pl.pallas_call(
        functools.partial(kernel, cores, subj_n, vox_n, chunk, own * subj_n),
        out_shape=(
            jax.ShapeDtypeStruct((own, features, frames), f32),
            jax.ShapeDtypeStruct((features, frames), f32),
        ),
        in_specs=[hbm, vmem],
        out_specs=(hbm, vmem),
        scratch_shapes=[
            pltpu.VMEM((own, frames, voxels), bf16),
            pltpu.VMEM((frames, frames), f32),
            pltpu.VMEM((own, vox_n * chunk, LANES), f32),
            pltpu.VMEM((own, vox_n - 1, chunk, LANES), f32),
            pltpu.VMEM((own, vox_n * chunk, LANES), f32),
            pltpu.VMEM((OUTER, tile_n, ROWS, LANES), f32),
            pltpu.VMEM((OUTER, subj_n, ROWS, LANES), f32),
            pltpu.VMEM((tile_n, ROWS, LANES), bf16),
            pltpu.VMEM((tile_n, ROWS, LANES), f32),
            pltpu.VMEM((own, features, frames), f32),
            dma((own, PIECES)),
            dma,
            dma((own, vox_n - 1)),
            dma((own, vox_n - 1)),
            dma((own, vox_n - 1)),
            dma((own, vox_n - 1)),
            dma((OUTER, subj_n - 1)),
            dma((OUTER, subj_n - 1)),
            dma((chips - 1,)),
            dma((chips - 1,)),
            dma((chips - 1,)),
            dma((chips - 1,)),
        ],
        compiler_params=pltpu.CompilerParams(
            collective_id=0, has_side_effects=True, vmem_limit_bytes=32 * 1024 * 1024
        ),
        cost_estimate=pl.CostEstimate(
            flops=flops, bytes_accessed=data.size * 2, transcendentals=0
        ),
    )(data, shared_start)


def solution(mesh):
    placed = (P("subj", None, "vox"), P())
    body = functools.partial(local, mesh.shape["subj"], mesh.shape["vox"])
    return jax.shard_map(
        body, mesh=mesh, in_specs=placed, out_specs=(P("subj", None, None), P()), check_vma=False
    )
```

```python
import functools

import jax
import jax.numpy as jnp
from jax import lax
from jax.experimental import pallas as pl
from jax.experimental.pallas import tpu as pltpu
from jax.sharding import PartitionSpec as P

OUTER = 2
LANES = 128
ROWS = 16
PIECES = 1
MESH = pl.DeviceIdType.MESH


def each(start, stop, body):
    if stop - start <= 16:
        for step in range(start, stop):
            body(step)
    else:

        def looped(step, carry):
            body(step)
            return carry

        lax.fori_loop(start, stop, looped, 0)


def halves(x):
    high = x.astype(jnp.bfloat16)
    low = (x - high.astype(jnp.float32)).astype(jnp.bfloat16)
    return high, low


def dot(x, y):
    return jnp.dot(x, y, preferred_element_type=jnp.float32)


def dot_t(x, y):
    return lax.dot_general(x, y, (((1,), (1,)), ((), ())), preferred_element_type=jnp.float32)


def product(x, y):
    x_high, x_low = x
    y_high, y_low = y
    wide = jnp.concatenate([x_high, x_low], axis=1)
    tall = jnp.concatenate([y_high, y_high], axis=0)
    return dot(wide, tall) + dot(x_high, y_low)


def chain(shared, grams):
    features = shared.shape[0]
    row = lax.broadcasted_iota(jnp.int32, (features, features), 0)
    col = lax.broadcasted_iota(jnp.int32, (features, features), 1)
    left = [dot(shared, high) + dot(shared, low) for high, low in grams]
    left2 = [halves(x) for x in left]
    first = [dot_t(high, shared) + dot_t(low, shared) for high, low in left2]
    squares = [jnp.sum(jnp.where(row == col, x, 0.0), keepdims=True) + 1e-06 for x in first]
    gram = [x * (1.0 / s) for x, s in zip(first, squares)]
    gram2 = [halves(x) for x in gram]
    for last in (False, False, True):
        if not last:
            square = [product(x, x) for x in gram2]
        left = [1.5 * x - 0.5 * product(g, y) for x, g, y in zip(left, gram2, left2)]
        if not last:
            square2 = [halves(x) for x in square]
            gram = [
                2.25 * g - 1.5 * q + 0.25 * product(g2, q2)
                for g, q, g2, q2 in zip(gram, square, gram2, square2)
            ]
            gram2 = [halves(x) for x in gram]
            left2 = [halves(x) for x in left]
    return [x * lax.rsqrt(s) for x, s in zip(left, squares)]


def pack(gram, frames, total_rows):
    rest = frames - LANES
    row = lax.broadcasted_iota(jnp.int32, (LANES, LANES), 0)
    col = lax.broadcasted_iota(jnp.int32, (LANES, LANES), 1)
    corner = gram[LANES:, LANES:]
    corner = jnp.concatenate([corner, jnp.zeros((rest, LANES - rest), jnp.float32)], axis=1)
    corner = jnp.concatenate([corner, jnp.zeros((LANES - rest, LANES), jnp.float32)], axis=0)
    corner = pltpu.roll(corner, 1, 1)
    parts = [jnp.where(row >= col, gram[:LANES, :LANES], corner), gram[LANES:, :LANES]]
    if total_rows > frames:
        parts.append(jnp.zeros((total_rows - frames, LANES), jnp.float32))
    return jnp.concatenate(parts, axis=0)


def unpack(packed, frames):
    rest = frames - LANES
    row = lax.broadcasted_iota(jnp.int32, (LANES, LANES), 0)
    col = lax.broadcasted_iota(jnp.int32, (LANES, LANES), 1)
    both = packed[:LANES]
    cross = packed[LANES:frames]
    cross = jnp.concatenate([cross, jnp.zeros((LANES - rest, LANES), jnp.float32)], axis=0)
    top = jnp.where(row >= col, both, both.T)
    rolled = pltpu.roll(both, LANES - 1, 1)
    corner = jnp.where(col >= row, rolled, rolled.T)
    corner = jnp.where((row < rest) & (col < rest), corner, 0.0)
    return jnp.concatenate(
        [jnp.concatenate([top, cross.T], axis=1), jnp.concatenate([cross, corner], axis=1)], axis=0
    )


def kernel(
    cores, subj_n, vox_n, chunk, subjects,
    data_ref, shared_ref, proj_ref, resp_ref,
    held, acc, packed, parts, gathered, tiles, sums, shares, pieces,
    load_sem, rs_send, rs_recv, ag_send, ag_recv, sum_send, sum_recv, share_send, share_recv,
    piece_send, piece_recv,
):
    own, frames, voxels = data_ref.shape
    features = shared_ref.shape[1]
    s = lax.axis_index("subj")
    v = lax.axis_index("vox")
    z = s // cores
    core = s % cores
    planes = subj_n // cores
    chips = planes * vox_n
    chip = z * vox_n + v
    tile_n = (features // ROWS) * 2
    mine = chip

    def remember(count, work):
        known = [None] + [work(step) for step in range(1, count)] if count <= 17 else None
        return lambda step: known[step] if known else work(step)

    def chip_at(step):
        other = lax.rem(chip + step, chips)
        return (other // vox_n * cores + core, lax.rem(other, vox_n))

    subj_device = remember(subj_n, lambda step: (lax.rem(s + step, subj_n), v))
    chip_device = remember(chips, chip_at)
    vox_device = remember(vox_n, lambda step: (s, lax.rem(v + step, vox_n)))
    tile_of = remember(
        subj_n,
        lambda step: jnp.minimum(lax.rem(s + step, subj_n) // cores * vox_n + v, tile_n - 1),
    )

    width = voxels // PIECES
    loads = []
    for i in range(own):
        for p in range(PIECES):
            cut = pl.ds(p * width, width)
            load = pltpu.make_async_copy(
                data_ref.at[i, :, cut], held.at[i, :, cut], load_sem.at[i, p]
            )
            load.start()
            loads.append(load)

    barrier = pltpu.get_barrier_semaphore()

    def greet_subj(step):
        pl.semaphore_signal(barrier, inc=1, device_id=subj_device(step), device_id_type=MESH)

    def greet_chip(step):
        pl.semaphore_signal(barrier, inc=1, device_id=chip_device(step), device_id_type=MESH)

    each(1, subj_n, greet_subj)
    each(1, chips, greet_chip)

    shared = shared_ref[...].astype(jnp.float32).T.astype(jnp.bfloat16)
    pad = jnp.zeros((features, 2 * LANES - frames), jnp.bfloat16)
    shared = jnp.concatenate([shared, pad], axis=1)

    def scatter(i, step):
        other = lax.rem(v + step, vox_n)
        return pltpu.make_async_remote_copy(
            src_ref=packed.at[i, pl.ds(pl.multiple_of(other * chunk, 8), chunk)],
            dst_ref=parts.at[i, step - 1],
            send_sem=rs_send.at[i, step - 1],
            recv_sem=rs_recv.at[i, step - 1],
            device_id=vox_device(step),
            device_id_type=MESH,
        )

    def gather(i, step):
        cut = pl.ds(pl.multiple_of(v * chunk, 8), chunk)
        return pltpu.make_async_remote_copy(
            src_ref=gathered.at[i, cut],
            dst_ref=gathered.at[i, cut],
            send_sem=ag_send.at[i, step - 1],
            recv_sem=ag_recv.at[i, step - 1],
            device_id=vox_device(step),
            device_id_type=MESH,
        )

    def sum_copy(o, step):
        tile = tile_of(step)
        return pltpu.make_async_remote_copy(
            src_ref=tiles.at[o, tile],
            dst_ref=sums.at[o, s],
            send_sem=sum_send.at[o, step - 1],
            recv_sem=sum_recv.at[o, step - 1],
            device_id=subj_device(step),
            device_id_type=MESH,
        )

    def share_copy(o, step):
        ref = pieces if o else shares
        tile = jnp.minimum(mine, tile_n - 1)
        return pltpu.make_async_remote_copy(
            src_ref=ref.at[tile],
            dst_ref=ref.at[tile],
            send_sem=(piece_send if o else share_send).at[step - 1],
            recv_sem=(piece_recv if o else share_recv).at[step - 1],
            device_id=chip_device(step),
            device_id_type=MESH,
        )

    def when(condition, body):
        if chips <= tile_n:
            body()
        else:
            pl.when(condition)(body)

    for i in range(own):
        for p in range(PIECES):
            loads[i * PIECES + p].wait()
            piece = held[i, :, p * width : (p + 1) * width]
            if p == 0:
                acc[...] = dot_t(piece, piece)
            else:
                acc[...] += dot_t(piece, piece)
        packed[i] = pack(acc[...], frames, vox_n * chunk)
        if i == 0:
            pl.semaphore_wait(barrier, subj_n - 1 + chips - 1)
        each(1, vox_n, lambda step: scatter(i, step).start())

    for i in range(own):
        each(1, vox_n, lambda step: scatter(i, step).wait_recv())
        total = packed[i, pl.ds(pl.multiple_of(v * chunk, 8), chunk)]
        for step in range(1, vox_n):
            total = total + parts[i, step - 1]
        gathered[i, pl.ds(pl.multiple_of(v * chunk, 8), chunk)] = total
        each(1, vox_n, lambda step: gather(i, step).start())

    grams = []
    for i in range(own):
        each(1, vox_n, lambda step: gather(i, step).wait_recv())
        grams.append(halves(unpack(gathered[i], frames)))

    for o in range(OUTER):
        projections = chain(shared, grams)
        total = projections[0]
        for other in projections[1:]:
            total = total + other
        for j in range(tile_n):
            tiles[o, j] = total[
                j // 2 * ROWS : (j // 2 + 1) * ROWS, j % 2 * LANES : (j % 2 + 1) * LANES
            ]

        def send_sum(step):
            other = lax.rem(s + step, subj_n)
            when(
                other // cores * vox_n + v < tile_n,
                lambda: sum_copy(o, step).start(),
            )

        each(1, subj_n, send_sum)
        if o == OUTER - 1:
            for i in range(own):
                proj_ref[i] = projections[i].T[:frames]

        def reduce():
            sums[o, s] = tiles[o, mine]
            each(1, subj_n, lambda step: sum_copy(o, step).wait_recv())
            summed = sums[o, 0]
            for q in range(1, subj_n):
                summed = summed + sums[o, q]
            mean = summed / jnp.float32(subjects)
            if o == OUTER - 1:
                pieces[mine] = mean
            else:
                shares[mine] = mean.astype(jnp.bfloat16)
            each(1, chips, lambda step: share_copy(o, step).start())

        when(mine < tile_n, reduce)

        def wait_share(step):
            other = lax.rem(chip + chips - step, chips)
            when(other < tile_n, lambda: share_copy(o, step).wait_recv())

        each(1, chips, wait_share)
        ref = pieces if o == OUTER - 1 else shares
        shared = jnp.concatenate(
            [
                jnp.concatenate([ref[2 * a], ref[2 * a + 1]], axis=1)
                for a in range(tile_n // 2)
            ],
            axis=0,
        )
    resp_ref[...] = shared.T[:frames]

    for i in range(own):
        each(1, vox_n, lambda step: scatter(i, step).wait_send())
        each(1, vox_n, lambda step: gather(i, step).wait_send())
    for o in range(OUTER):

        def sent_sum(step):
            other = lax.rem(s + step, subj_n)
            when(
                other // cores * vox_n + v < tile_n,
                lambda: sum_copy(o, step).wait_send(),
            )

        each(1, subj_n, sent_sum)
        when(
            mine < tile_n,
            lambda: each(1, chips, lambda step: share_copy(o, step).wait_send()),
        )


def local(subj_n, vox_n, data, shared_start):
    own, frames, voxels = data.shape
    features = shared_start.shape[0]
    cores = 2
    chips = subj_n // cores * vox_n
    tile_n = features // ROWS * 2
    assert chips >= tile_n and tile_n % vox_n == 0
    chunk = -(-frames // (8 * vox_n)) * 8
    hbm = pl.BlockSpec(memory_space=pltpu.HBM)
    vmem = pl.BlockSpec(memory_space=pltpu.VMEM)
    f32, bf16 = jnp.float32, jnp.bfloat16
    dma = pltpu.SemaphoreType.DMA
    flops = 2 * own * frames * frames * voxels
    projections, response = pl.pallas_call(
        functools.partial(kernel, cores, subj_n, vox_n, chunk, own * subj_n),
        out_shape=(
            jax.ShapeDtypeStruct((own, frames, features), f32),
            jax.ShapeDtypeStruct((frames, features), f32),
        ),
        in_specs=[hbm, vmem],
        out_specs=(vmem, vmem),
        scratch_shapes=[
            pltpu.VMEM((own, frames, voxels), bf16),
            pltpu.VMEM((frames, frames), f32),
            pltpu.VMEM((own, vox_n * chunk, LANES), f32),
            pltpu.VMEM((own, vox_n - 1, chunk, LANES), f32),
            pltpu.VMEM((own, vox_n * chunk, LANES), f32),
            pltpu.VMEM((OUTER, tile_n, ROWS, LANES), f32),
            pltpu.VMEM((OUTER, subj_n, ROWS, LANES), f32),
            pltpu.VMEM((tile_n, ROWS, LANES), bf16),
            pltpu.VMEM((tile_n, ROWS, LANES), f32),
            dma((own, PIECES)),
            dma((own, vox_n - 1)),
            dma((own, vox_n - 1)),
            dma((own, vox_n - 1)),
            dma((own, vox_n - 1)),
            dma((OUTER, subj_n - 1)),
            dma((OUTER, subj_n - 1)),
            dma((chips - 1,)),
            dma((chips - 1,)),
            dma((chips - 1,)),
            dma((chips - 1,)),
        ],
        compiler_params=pltpu.CompilerParams(
            collective_id=0, has_side_effects=True, vmem_limit_bytes=52 * 2**20
        ),
        cost_estimate=pl.CostEstimate(
            flops=flops, bytes_accessed=data.size * 2, transcendentals=0
        ),
    )(data, shared_start.T)
    return projections.transpose(0, 2, 1), response.T


def solution(mesh):
    placed = (P("subj", None, "vox"), P())
    body = functools.partial(local, mesh.shape["subj"], mesh.shape["vox"])
    return jax.shard_map(
        body, mesh=mesh, in_specs=placed, out_specs=(P("subj", None, None), P()), check_vma=False
    )
```

```python
import functools

import jax
import jax.numpy as jnp
from jax import lax
from jax.experimental import pallas as pl
from jax.experimental.pallas import tpu as pltpu
from jax.sharding import PartitionSpec as P

OUTER = 2
LANES = 128
ROWS = 16
PIECES = 1
MESH = pl.DeviceIdType.MESH


def each(start, stop, body):
    if stop - start <= 16:
        for step in range(start, stop):
            body(step)
    else:

        def looped(step, carry):
            body(step)
            return carry

        lax.fori_loop(start, stop, looped, 0)


def halves(x):
    high = x.astype(jnp.bfloat16)
    low = (x - high.astype(jnp.float32)).astype(jnp.bfloat16)
    return high, low


def dot(x, y):
    return jnp.dot(x, y, preferred_element_type=jnp.float32)


def dot_t(x, y):
    return lax.dot_general(x, y, (((1,), (1,)), ((), ())), preferred_element_type=jnp.float32)


def product(x, y):
    x_high, x_low = x
    y_high, y_low = y
    wide = jnp.concatenate([x_high, x_low], axis=1)
    tall = jnp.concatenate([y_high, y_high], axis=0)
    return dot(wide, tall) + dot(x_high, y_low)


def chain(shared, grams):
    features = shared.shape[0]
    row = lax.broadcasted_iota(jnp.int32, (features, features), 0)
    col = lax.broadcasted_iota(jnp.int32, (features, features), 1)
    left = [dot(shared, high) + dot(shared, low) for high, low in grams]
    left2 = [halves(x) for x in left]
    first = [dot_t(high, shared) + dot_t(low, shared) for high, low in left2]
    squares = [jnp.sum(jnp.where(row == col, x, 0.0), keepdims=True) + 1e-06 for x in first]
    gram = [x * (1.0 / s) for x, s in zip(first, squares)]
    gram2 = [halves(x) for x in gram]
    for last in (False, False, True):
        if not last:
            square = [product(x, x) for x in gram2]
        left = [1.5 * x - 0.5 * product(g, y) for x, g, y in zip(left, gram2, left2)]
        if not last:
            square2 = [halves(x) for x in square]
            gram = [
                2.25 * g - 1.5 * q + 0.25 * product(g2, q2)
                for g, q, g2, q2 in zip(gram, square, gram2, square2)
            ]
            gram2 = [halves(x) for x in gram]
            left2 = [halves(x) for x in left]
    return [x * lax.rsqrt(s) for x, s in zip(left, squares)]


def pack(gram, frames, total_rows):
    rest = frames - LANES
    row = lax.broadcasted_iota(jnp.int32, (LANES, LANES), 0)
    col = lax.broadcasted_iota(jnp.int32, (LANES, LANES), 1)
    corner = gram[LANES:, LANES:]
    corner = jnp.concatenate([corner, jnp.zeros((rest, LANES - rest), jnp.float32)], axis=1)
    corner = jnp.concatenate([corner, jnp.zeros((LANES - rest, LANES), jnp.float32)], axis=0)
    corner = pltpu.roll(corner, 1, 1)
    parts = [jnp.where(row >= col, gram[:LANES, :LANES], corner), gram[LANES:, :LANES]]
    if total_rows > frames:
        parts.append(jnp.zeros((total_rows - frames, LANES), jnp.float32))
    return jnp.concatenate(parts, axis=0)


def unpack(packed, frames):
    rest = frames - LANES
    row = lax.broadcasted_iota(jnp.int32, (LANES, LANES), 0)
    col = lax.broadcasted_iota(jnp.int32, (LANES, LANES), 1)
    both = packed[:LANES]
    cross = packed[LANES:frames]
    cross = jnp.concatenate([cross, jnp.zeros((LANES - rest, LANES), jnp.float32)], axis=0)
    top = jnp.where(row >= col, both, both.T)
    rolled = pltpu.roll(both, LANES - 1, 1)
    corner = jnp.where(col >= row, rolled, rolled.T)
    corner = jnp.where((row < rest) & (col < rest), corner, 0.0)
    return jnp.concatenate(
        [jnp.concatenate([top, cross.T], axis=1), jnp.concatenate([cross, corner], axis=1)], axis=0
    )


def kernel(
    cores, subj_n, vox_n, chunk, subjects,
    data_ref, shared_ref, proj_ref, resp_ref,
    held, acc, packed, parts, gathered, tiles, pair, sums, shares, pieces,
    load_sem, rs_send, rs_recv, ag_send, ag_recv, pair_send, pair_recv, sum_send, sum_recv, share_send, share_recv,
    piece_send, piece_recv,
):
    own, frames, voxels = data_ref.shape
    features = shared_ref.shape[1]
    s = lax.axis_index("subj")
    v = lax.axis_index("vox")
    z = s // cores
    core = s % cores
    planes = subj_n // cores
    tile_n = (features // ROWS) * 2
    block_n = tiles.shape[1]
    joined = tile_n // block_n
    plane_n = vox_n * cores
    place = v * cores + core
    mine = jnp.minimum(place, block_n - 1)
    theirs = jnp.minimum(v * cores + 1 - core, block_n - 1)

    def remember(count, work):
        known = [None] + [work(step) for step in range(1, count)] if count <= 17 else None
        return lambda step: known[step] if known else work(step)

    def plane_at(step):
        other = lax.rem(place + step, plane_n)
        return (z * cores + lax.rem(other, cores), other // cores)

    plane_device = remember(plane_n, plane_at)
    depth_device = remember(
        planes, lambda step: (lax.rem(z + step, planes) * cores + core, v)
    )
    vox_device = remember(vox_n, lambda step: (s, lax.rem(v + step, vox_n)))
    pair_device = (z * cores + 1 - core, v)

    width = voxels // PIECES
    loads = []
    for i in range(own):
        for p in range(PIECES):
            cut = pl.ds(p * width, width)
            load = pltpu.make_async_copy(
                data_ref.at[i, :, cut], held.at[i, :, cut], load_sem.at[i, p]
            )
            load.start()
            loads.append(load)

    barrier = pltpu.get_barrier_semaphore()

    def greet_plane(step):
        pl.semaphore_signal(barrier, inc=1, device_id=plane_device(step), device_id_type=MESH)

    def greet_depth(step):
        pl.semaphore_signal(barrier, inc=1, device_id=depth_device(step), device_id_type=MESH)

    each(1, plane_n, greet_plane)
    each(1, planes, greet_depth)

    shared = shared_ref[...].astype(jnp.float32).T.astype(jnp.bfloat16)
    pad = jnp.zeros((features, 2 * LANES - frames), jnp.bfloat16)
    shared = jnp.concatenate([shared, pad], axis=1)

    def scatter(i, step):
        other = lax.rem(v + step, vox_n)
        return pltpu.make_async_remote_copy(
            src_ref=packed.at[i, pl.ds(pl.multiple_of(other * chunk, 8), chunk)],
            dst_ref=parts.at[i, step - 1],
            send_sem=rs_send.at[i, step - 1],
            recv_sem=rs_recv.at[i, step - 1],
            device_id=vox_device(step),
            device_id_type=MESH,
        )

    def gather(i, step):
        cut = pl.ds(pl.multiple_of(v * chunk, 8), chunk)
        return pltpu.make_async_remote_copy(
            src_ref=gathered.at[i, cut],
            dst_ref=gathered.at[i, cut],
            send_sem=ag_send.at[i, step - 1],
            recv_sem=ag_recv.at[i, step - 1],
            device_id=vox_device(step),
            device_id_type=MESH,
        )

    def pair_copy(o):
        return pltpu.make_async_remote_copy(
            src_ref=tiles.at[o, theirs],
            dst_ref=pair.at[o],
            send_sem=pair_send.at[o],
            recv_sem=pair_recv.at[o],
            device_id=pair_device,
            device_id_type=MESH,
        )

    def depth_copy(o, step):
        return pltpu.make_async_remote_copy(
            src_ref=sums.at[o, z],
            dst_ref=sums.at[o, z],
            send_sem=sum_send.at[o, step - 1],
            recv_sem=sum_recv.at[o, step - 1],
            device_id=depth_device(step),
            device_id_type=MESH,
        )

    def share_copy(o, step):
        ref = pieces if o else shares
        return pltpu.make_async_remote_copy(
            src_ref=ref.at[mine],
            dst_ref=ref.at[mine],
            send_sem=(piece_send if o else share_send).at[step - 1],
            recv_sem=(piece_recv if o else share_recv).at[step - 1],
            device_id=plane_device(step),
            device_id_type=MESH,
        )

    def when(condition, body):
        if plane_n <= block_n:
            body()
        else:
            pl.when(condition)(body)

    for i in range(own):
        for p in range(PIECES):
            loads[i * PIECES + p].wait()
            piece = held[i, :, p * width : (p + 1) * width]
            if p == 0:
                acc[...] = dot_t(piece, piece)
            else:
                acc[...] += dot_t(piece, piece)
        packed[i] = pack(acc[...], frames, vox_n * chunk)
        if i == 0:
            pl.semaphore_wait(barrier, plane_n - 1 + planes - 1)
        each(1, vox_n, lambda step: scatter(i, step).start())

    for i in range(own):
        each(1, vox_n, lambda step: scatter(i, step).wait_recv())
        total = packed[i, pl.ds(pl.multiple_of(v * chunk, 8), chunk)]
        for step in range(1, vox_n):
            total = total + parts[i, step - 1]
        gathered[i, pl.ds(pl.multiple_of(v * chunk, 8), chunk)] = total
        each(1, vox_n, lambda step: gather(i, step).start())

    grams = []
    for i in range(own):
        each(1, vox_n, lambda step: gather(i, step).wait_recv())
        grams.append(halves(unpack(gathered[i], frames)))

    def piece_of(ref, j):
        return ref[j // joined, j % joined * ROWS : (j % joined + 1) * ROWS]

    for o in range(OUTER):
        projections = chain(shared, grams)
        total = projections[0]
        for other in projections[1:]:
            total = total + other
        for j in range(tile_n):
            tiles[o, j // joined, j % joined * ROWS : (j % joined + 1) * ROWS] = total[
                j // 2 * ROWS : (j // 2 + 1) * ROWS, j % 2 * LANES : (j % 2 + 1) * LANES
            ]

        when(place < block_n, lambda: pair_copy(o).start())
        def stack():
            pair_copy(o).wait_recv()
            sums[o, z] = tiles[o, mine] + pair[o]
            each(1, planes, lambda step: depth_copy(o, step).start())

        when(place < block_n, stack)
        if o == OUTER - 1:
            for i in range(own):
                proj_ref[i] = projections[i].T[:frames]

        def reduce():
            each(1, planes, lambda step: depth_copy(o, step).wait_recv())
            summed = sums[o, 0]
            for q in range(1, planes):
                summed = summed + sums[o, q]
            mean = summed / jnp.float32(subjects)
            if o == OUTER - 1:
                pieces[mine] = mean
            else:
                shares[mine] = mean.astype(jnp.bfloat16)
            each(1, plane_n, lambda step: share_copy(o, step).start())

        when(place < block_n, reduce)

        def wait_share(step):
            other = lax.rem(place + plane_n - step, plane_n)
            when(other < block_n, lambda: share_copy(o, step).wait_recv())

        each(1, plane_n, wait_share)
        ref = pieces if o == OUTER - 1 else shares
        shared = jnp.concatenate(
            [
                jnp.concatenate([piece_of(ref, 2 * a), piece_of(ref, 2 * a + 1)], axis=1)
                for a in range(tile_n // 2)
            ],
            axis=0,
        )
    resp_ref[...] = shared.T[:frames]

    for i in range(own):
        each(1, vox_n, lambda step: scatter(i, step).wait_send())
        each(1, vox_n, lambda step: gather(i, step).wait_send())
    for o in range(OUTER):

        def sent():
            pair_copy(o).wait_send()
            each(1, planes, lambda step: depth_copy(o, step).wait_send())
            each(1, plane_n, lambda step: share_copy(o, step).wait_send())

        when(place < block_n, sent)


def local(subj_n, vox_n, data, shared_start):
    own, frames, voxels = data.shape
    features = shared_start.shape[0]
    cores = 2
    planes = subj_n // cores
    plane_n = vox_n * cores
    tile_n = features // ROWS * 2
    joined = max(1, tile_n // plane_n)
    assert tile_n % joined == 0 and tile_n // joined <= plane_n
    blocks = (tile_n // joined, joined * ROWS, LANES)
    chunk = -(-frames // (8 * vox_n)) * 8
    hbm = pl.BlockSpec(memory_space=pltpu.HBM)
    vmem = pl.BlockSpec(memory_space=pltpu.VMEM)
    f32, bf16 = jnp.float32, jnp.bfloat16
    dma = pltpu.SemaphoreType.DMA
    flops = 2 * own * frames * frames * voxels
    projections, response = pl.pallas_call(
        functools.partial(kernel, cores, subj_n, vox_n, chunk, own * subj_n),
        out_shape=(
            jax.ShapeDtypeStruct((own, frames, features), f32),
            jax.ShapeDtypeStruct((frames, features), f32),
        ),
        in_specs=[hbm, vmem],
        out_specs=(vmem, vmem),
        scratch_shapes=[
            pltpu.VMEM((own, frames, voxels), bf16),
            pltpu.VMEM((frames, frames), f32),
            pltpu.VMEM((own, vox_n * chunk, LANES), f32),
            pltpu.VMEM((own, vox_n - 1, chunk, LANES), f32),
            pltpu.VMEM((own, vox_n * chunk, LANES), f32),
            pltpu.VMEM((OUTER, *blocks), f32),
            pltpu.VMEM((OUTER, *blocks[1:]), f32),
            pltpu.VMEM((OUTER, planes, *blocks[1:]), f32),
            pltpu.VMEM(blocks, bf16),
            pltpu.VMEM(blocks, f32),
            dma((own, PIECES)),
            dma((own, vox_n - 1)),
            dma((own, vox_n - 1)),
            dma((own, vox_n - 1)),
            dma((own, vox_n - 1)),
            dma((OUTER,)),
            dma((OUTER,)),
            dma((OUTER, planes - 1)),
            dma((OUTER, planes - 1)),
            dma((plane_n - 1,)),
            dma((plane_n - 1,)),
            dma((plane_n - 1,)),
            dma((plane_n - 1,)),
        ],
        compiler_params=pltpu.CompilerParams(
            collective_id=0, has_side_effects=True, vmem_limit_bytes=52 * 2**20
        ),
        cost_estimate=pl.CostEstimate(
            flops=flops, bytes_accessed=data.size * 2, transcendentals=0
        ),
    )(data, shared_start.T)
    return projections.transpose(0, 2, 1), response.T


def solution(mesh):
    placed = (P("subj", None, "vox"), P())
    body = functools.partial(local, mesh.shape["subj"], mesh.shape["vox"])
    return jax.shard_map(
        body, mesh=mesh, in_specs=placed, out_specs=(P("subj", None, None), P()), check_vma=False
    )
```

```python
import functools

import jax
import jax.numpy as jnp
from jax import lax
from jax.experimental import pallas as pl
from jax.experimental.pallas import tpu as pltpu
from jax.sharding import PartitionSpec as P

OUTER = 2
LANES = 128
ROWS = 16
PIECES = 1
MESH = pl.DeviceIdType.MESH


def each(start, stop, body):
    if stop - start <= 16:
        for step in range(start, stop):
            body(step)
    else:

        def looped(step, carry):
            body(step)
            return carry

        lax.fori_loop(start, stop, looped, 0)


def halves(x):
    high = x.astype(jnp.bfloat16)
    low = (x - high.astype(jnp.float32)).astype(jnp.bfloat16)
    return high, low


def dot(x, y):
    return jnp.dot(x, y, preferred_element_type=jnp.float32)


def dot_t(x, y):
    return lax.dot_general(x, y, (((1,), (1,)), ((), ())), preferred_element_type=jnp.float32)


def product(x, y):
    x_high, x_low = x
    y_high, y_low = y
    wide = jnp.concatenate([x_high, x_low], axis=1)
    tall = jnp.concatenate([y_high, y_high], axis=0)
    return dot(wide, tall) + dot(x_high, y_low)


def chain(shared, grams):
    features = shared.shape[0]
    row = lax.broadcasted_iota(jnp.int32, (features, features), 0)
    col = lax.broadcasted_iota(jnp.int32, (features, features), 1)
    left = [dot(shared, high) + dot(shared, low) for high, low in grams]
    left2 = [halves(x) for x in left]
    first = [dot_t(high, shared) + dot_t(low, shared) for high, low in left2]
    squares = [jnp.sum(jnp.where(row == col, x, 0.0), keepdims=True) + 1e-06 for x in first]
    gram = [x * (1.0 / s) for x, s in zip(first, squares)]
    gram2 = [halves(x) for x in gram]
    for last in (False, False, True):
        if not last:
            square = [product(x, x) for x in gram2]
        left = [1.5 * x - 0.5 * product(g, y) for x, g, y in zip(left, gram2, left2)]
        if not last:
            square2 = [halves(x) for x in square]
            gram = [
                2.25 * g - 1.5 * q + 0.25 * product(g2, q2)
                for g, q, g2, q2 in zip(gram, square, gram2, square2)
            ]
            gram2 = [halves(x) for x in gram]
            left2 = [halves(x) for x in left]
    return [x * lax.rsqrt(s) for x, s in zip(left, squares)]


def pack(gram, frames, total_rows):
    rest = frames - LANES
    row = lax.broadcasted_iota(jnp.int32, (LANES, LANES), 0)
    col = lax.broadcasted_iota(jnp.int32, (LANES, LANES), 1)
    corner = gram[LANES:, LANES:]
    corner = jnp.concatenate([corner, jnp.zeros((rest, LANES - rest), jnp.float32)], axis=1)
    corner = jnp.concatenate([corner, jnp.zeros((LANES - rest, LANES), jnp.float32)], axis=0)
    corner = pltpu.roll(corner, 1, 1)
    parts = [jnp.where(row >= col, gram[:LANES, :LANES], corner), gram[LANES:, :LANES]]
    if total_rows > frames:
        parts.append(jnp.zeros((total_rows - frames, LANES), jnp.float32))
    return jnp.concatenate(parts, axis=0)


def unpack(packed, frames):
    rest = frames - LANES
    row = lax.broadcasted_iota(jnp.int32, (LANES, LANES), 0)
    col = lax.broadcasted_iota(jnp.int32, (LANES, LANES), 1)
    both = packed[:LANES]
    cross = packed[LANES:frames]
    cross = jnp.concatenate([cross, jnp.zeros((LANES - rest, LANES), jnp.float32)], axis=0)
    top = jnp.where(row >= col, both, both.T)
    rolled = pltpu.roll(both, LANES - 1, 1)
    corner = jnp.where(col >= row, rolled, rolled.T)
    corner = jnp.where((row < rest) & (col < rest), corner, 0.0)
    return jnp.concatenate(
        [jnp.concatenate([top, cross.T], axis=1), jnp.concatenate([cross, corner], axis=1)], axis=0
    )


def kernel(
    cores, subj_n, vox_n, chunk, subjects,
    data_ref, shared_ref, proj_ref, resp_ref,
    held, acc, packed, parts, gathered, tiles, pair, sums, shares, pieces,
    load_sem, rs_send, rs_recv, ag_send, ag_recv, pair_send, pair_recv, sum_send, sum_recv, share_send, share_recv,
    piece_send, piece_recv,
):
    own, frames, voxels = data_ref.shape
    features = shared_ref.shape[1]
    s = lax.axis_index("subj")
    v = lax.axis_index("vox")
    z = s // cores
    core = s % cores
    planes = subj_n // cores
    tile_n = (features // ROWS) * 2
    block_n = tiles.shape[1]
    joined = tile_n // block_n
    plane_n = vox_n * cores
    place = v * cores + core
    mine = jnp.minimum(place, block_n - 1)
    theirs = jnp.minimum(v * cores + 1 - core, block_n - 1)

    def remember(count, work):
        known = [None] + [work(step) for step in range(1, count)] if count <= 17 else None
        return lambda step: known[step] if known else work(step)

    def plane_at(step):
        other = lax.rem(place + step, plane_n)
        return (z * cores + lax.rem(other, cores), other // cores)

    plane_device = remember(plane_n, plane_at)
    depth_device = remember(
        planes, lambda step: (lax.rem(z + step, planes) * cores + core, v)
    )
    vox_device = remember(vox_n, lambda step: (s, lax.rem(v + step, vox_n)))
    pair_device = (z * cores + 1 - core, v)

    width = voxels // PIECES
    loads = []
    for i in range(own):
        for p in range(PIECES):
            cut = pl.ds(p * width, width)
            load = pltpu.make_async_copy(
                data_ref.at[i, :, cut], held.at[i, :, cut], load_sem.at[i, p]
            )
            load.start()
            loads.append(load)

    barrier = pltpu.get_barrier_semaphore()

    def greet_plane(step):
        pl.semaphore_signal(barrier, inc=1, device_id=plane_device(step), device_id_type=MESH)

    def greet_depth(step):
        pl.semaphore_signal(barrier, inc=1, device_id=depth_device(step), device_id_type=MESH)

    each(1, plane_n, greet_plane)
    each(1, planes, greet_depth)

    shared = shared_ref[...].astype(jnp.float32).T.astype(jnp.bfloat16)
    pad = jnp.zeros((features, 2 * LANES - frames), jnp.bfloat16)
    shared = jnp.concatenate([shared, pad], axis=1)

    def scatter(i, step):
        other = lax.rem(v + step, vox_n)
        return pltpu.make_async_remote_copy(
            src_ref=packed.at[i, pl.ds(pl.multiple_of(other * chunk, 8), chunk)],
            dst_ref=parts.at[i, step - 1],
            send_sem=rs_send.at[i, step - 1],
            recv_sem=rs_recv.at[i, step - 1],
            device_id=vox_device(step),
            device_id_type=MESH,
        )

    def gather(i, step):
        cut = pl.ds(pl.multiple_of(v * chunk, 8), chunk)
        return pltpu.make_async_remote_copy(
            src_ref=gathered.at[i, cut],
            dst_ref=gathered.at[i, cut],
            send_sem=ag_send.at[i, step - 1],
            recv_sem=ag_recv.at[i, step - 1],
            device_id=vox_device(step),
            device_id_type=MESH,
        )

    def pair_copy(o):
        return pltpu.make_async_remote_copy(
            src_ref=tiles.at[o, theirs],
            dst_ref=pair.at[o],
            send_sem=pair_send.at[o],
            recv_sem=pair_recv.at[o],
            device_id=pair_device,
            device_id_type=MESH,
        )

    def depth_copy(o, step):
        return pltpu.make_async_remote_copy(
            src_ref=sums.at[o, z],
            dst_ref=sums.at[o, z],
            send_sem=sum_send.at[o, step - 1],
            recv_sem=sum_recv.at[o, step - 1],
            device_id=depth_device(step),
            device_id_type=MESH,
        )

    def share_copy(o, step):
        ref = pieces if o else shares
        return pltpu.make_async_remote_copy(
            src_ref=ref.at[mine],
            dst_ref=ref.at[mine],
            send_sem=(piece_send if o else share_send).at[step - 1],
            recv_sem=(piece_recv if o else share_recv).at[step - 1],
            device_id=plane_device(step),
            device_id_type=MESH,
        )

    def when(condition, body):
        if plane_n <= block_n:
            body()
        else:
            pl.when(condition)(body)

    for i in range(own):
        for p in range(PIECES):
            loads[i * PIECES + p].wait()
            piece = held[i, :, p * width : (p + 1) * width]
            if p == 0:
                acc[...] = dot_t(piece, piece)
            else:
                acc[...] += dot_t(piece, piece)
        packed[i] = pack(acc[...], frames, vox_n * chunk)
        if i == 0:
            pl.semaphore_wait(barrier, plane_n - 1 + planes - 1)
        each(1, vox_n, lambda step: scatter(i, step).start())

    for i in range(own):
        each(1, vox_n, lambda step: scatter(i, step).wait_recv())
        total = packed[i, pl.ds(pl.multiple_of(v * chunk, 8), chunk)]
        for step in range(1, vox_n):
            total = total + parts[i, step - 1]
        gathered[i, pl.ds(pl.multiple_of(v * chunk, 8), chunk)] = total
        each(1, vox_n, lambda step: gather(i, step).start())

    grams = []
    for i in range(own):
        each(1, vox_n, lambda step: gather(i, step).wait_recv())
        grams.append(halves(unpack(gathered[i], frames)))

    def piece_of(ref, j):
        return ref[j // joined, j % joined * ROWS : (j % joined + 1) * ROWS]

    for o in range(OUTER):
        projections = chain(shared, grams)
        total = projections[0]
        for other in projections[1:]:
            total = total + other
        for j in range(tile_n):
            tiles[o, j // joined, j % joined * ROWS : (j % joined + 1) * ROWS] = total[
                j // 2 * ROWS : (j // 2 + 1) * ROWS, j % 2 * LANES : (j % 2 + 1) * LANES
            ]

        when(place < block_n, lambda: pair_copy(o).start())
        def stack():
            pair_copy(o).wait_recv()
            sums[o, z] = tiles[o, mine] + pair[o]
            each(1, planes, lambda step: depth_copy(o, step).start())

        when(place < block_n, stack)
        def reduce():
            each(1, planes, lambda step: depth_copy(o, step).wait_recv())
            summed = sums[o, 0]
            for q in range(1, planes):
                summed = summed + sums[o, q]
            mean = summed / jnp.float32(subjects)
            if o == OUTER - 1:
                pieces[mine] = mean
            else:
                shares[mine] = mean.astype(jnp.bfloat16)
            each(1, plane_n, lambda step: share_copy(o, step).start())

        when(place < block_n, reduce)

        def wait_share(step):
            other = lax.rem(place + plane_n - step, plane_n)
            when(other < block_n, lambda: share_copy(o, step).wait_recv())

        if o == OUTER - 1:
            for i in range(own):
                proj_ref[i] = projections[i].T[:frames]

        each(1, plane_n, wait_share)
        ref = pieces if o == OUTER - 1 else shares
        shared = jnp.concatenate(
            [
                jnp.concatenate([piece_of(ref, 2 * a), piece_of(ref, 2 * a + 1)], axis=1)
                for a in range(tile_n // 2)
            ],
            axis=0,
        )
    resp_ref[...] = shared.T[:frames]

    for i in range(own):
        each(1, vox_n, lambda step: scatter(i, step).wait_send())
        each(1, vox_n, lambda step: gather(i, step).wait_send())
    for o in range(OUTER):

        def sent():
            pair_copy(o).wait_send()
            each(1, planes, lambda step: depth_copy(o, step).wait_send())
            each(1, plane_n, lambda step: share_copy(o, step).wait_send())

        when(place < block_n, sent)


def local(subj_n, vox_n, data, shared_start):
    own, frames, voxels = data.shape
    features = shared_start.shape[0]
    cores = 2
    planes = subj_n // cores
    plane_n = vox_n * cores
    tile_n = features // ROWS * 2
    joined = max(1, tile_n // plane_n)
    assert tile_n % joined == 0 and tile_n // joined <= plane_n
    blocks = (tile_n // joined, joined * ROWS, LANES)
    chunk = -(-frames // (8 * vox_n)) * 8
    hbm = pl.BlockSpec(memory_space=pltpu.HBM)
    vmem = pl.BlockSpec(memory_space=pltpu.VMEM)
    f32, bf16 = jnp.float32, jnp.bfloat16
    dma = pltpu.SemaphoreType.DMA
    flops = 2 * own * frames * frames * voxels
    projections, response = pl.pallas_call(
        functools.partial(kernel, cores, subj_n, vox_n, chunk, own * subj_n),
        out_shape=(
            jax.ShapeDtypeStruct((own, frames, features), f32),
            jax.ShapeDtypeStruct((frames, features), f32),
        ),
        in_specs=[hbm, vmem],
        out_specs=(vmem, vmem),
        scratch_shapes=[
            pltpu.VMEM((own, frames, voxels), bf16),
            pltpu.VMEM((frames, frames), f32),
            pltpu.VMEM((own, vox_n * chunk, LANES), f32),
            pltpu.VMEM((own, vox_n - 1, chunk, LANES), f32),
            pltpu.VMEM((own, vox_n * chunk, LANES), f32),
            pltpu.VMEM((OUTER, *blocks), f32),
            pltpu.VMEM((OUTER, *blocks[1:]), f32),
            pltpu.VMEM((OUTER, planes, *blocks[1:]), f32),
            pltpu.VMEM(blocks, bf16),
            pltpu.VMEM(blocks, f32),
            dma((own, PIECES)),
            dma((own, vox_n - 1)),
            dma((own, vox_n - 1)),
            dma((own, vox_n - 1)),
            dma((own, vox_n - 1)),
            dma((OUTER,)),
            dma((OUTER,)),
            dma((OUTER, planes - 1)),
            dma((OUTER, planes - 1)),
            dma((plane_n - 1,)),
            dma((plane_n - 1,)),
            dma((plane_n - 1,)),
            dma((plane_n - 1,)),
        ],
        compiler_params=pltpu.CompilerParams(
            collective_id=0, has_side_effects=True, vmem_limit_bytes=52 * 2**20
        ),
        cost_estimate=pl.CostEstimate(
            flops=flops, bytes_accessed=data.size * 2, transcendentals=0
        ),
    )(data, shared_start.T)
    return projections.transpose(0, 2, 1), response.T


def solution(mesh):
    placed = (P("subj", None, "vox"), P())
    body = functools.partial(local, mesh.shape["subj"], mesh.shape["vox"])
    return jax.shard_map(
        body, mesh=mesh, in_specs=placed, out_specs=(P("subj", None, None), P()), check_vma=False
    )
```
